32 devices in a mesh: grp: 2 (over x), beam: 8 (over z, y), tp: 2 (over core).
Axes of the slice: x: 2, y: 2, z: 4, core: 2. Of those that a mesh axis runs over, the one named last changes fastest.
Arguments:
- queries: bfloat16 [256, 20, 128], P(('grp', 'beam'), 'tp'), parts along dimension 0, may hold values from -48 to 48
- new_entries: bfloat16 [256, 2, 4, 128], P(('grp', 'beam'), None, 'tp'), parts along dimension 0, may hold values from -6 to 6
- cache_pages: bfloat16 [768, 2, 4, 128, 128], P(('grp', 'beam'), None, 'tp'), parts along dimension 0, may hold values from -6 to 6
- cache_scales: bfloat16 [768, 2, 4], P(('grp', 'beam'), None, 'tp'), parts along dimension 0, may hold values from 0.5 to 2
- page_table: int32 [256, 3], P(('grp', 'beam')), parts along dimension 0, may hold values from 0 to 47, as said below
- lengths: int32 [256], P('grp'), parts along dimension 0, may hold values from 256 to 384, as said below
- parent: int32 [256], P('grp'), parts along dimension 0, may hold values from 0 to 127, as said below
- placement: int32 [256], P('grp'), parts along dimension 0, may hold values from 0 to 127, as said below
- out_weight: bfloat16 [2560, 2560], P('tp'), may hold values from -0.125 to 0.125
Outputs:
- mixed: bfloat16 [256, 2560], P(('grp', 'beam'), 'tp'), parts along dimension 0
The draws below stay inside these ranges and needn't reach their ends.
There are 2 independent parts, one for each index of `grp`. The reference program is written for one: setup_inputs(seed, part) draws one part's arguments, and reference() takes and returns one part's arrays. A program takes and returns all parts, laid end to end along the dimension named above; an argument that names none is the same for every part. Nothing has to cross between parts.
Inputs may be any that keep to these rules, and one draw needn't show every extreme that they name: `placement`: a permutation: each parent beam in its own slot. Among the children in the slots of one index of beam, at most 2 have their parent's slot on any one index of beam, and exactly 2 on some index; children may share a parent. `lengths`: multiples of 128; every index of beam holds a beam of length 384. `page_table`: the rows of the slots of one index of beam hold each of its page numbers 0 to 47 once.
All inputs are finite; a program needn't handle non-finite values.
Results may differ from the reference program's by a relative error of at most 0.0053.
Values may be sent and summed in bfloat16 or wider, within the bound.
No kernel may reach another device: no remote copies, remote signals or barrier semaphores. Data moves between devices by JAX's collectives and lax.ppermute only.
A program may use at most 128 MiB of HBM per device.

```python
import math
import jax
import jax.numpy as jnp
from jax import lax

DOUT = 2560
QH = 20
KVH = 4
HD = 128
PAGE = 128
P_MAX = 3
BEAM_DEV = 16
BEAMS = 128
POOL = 48
PAGES = 384


def shared_order(key):
    return jax.random.permutation(key, BEAMS).astype(jnp.int32)


def draw_placement(key, part):
    return shared_order(key)


def draw_parent(key, part):
    ordering = shared_order(key)
    key = jax.random.fold_in(key, 11)
    key_one, key_two = jax.random.split(key)
    devices = BEAMS // BEAM_DEV
    orderings = jax.vmap(lambda single: jax.random.permutation(single, devices))(jax.random.split(key_one, devices))
    column = jnp.arange(BEAM_DEV, dtype=jnp.int32) % devices
    source = orderings[:, column]
    local_slot = jax.random.randint(key_two, (devices, BEAM_DEV), 0, BEAM_DEV)
    slot_index = (source * BEAM_DEV + local_slot).reshape(BEAMS)
    inverse = jnp.argsort(ordering)
    return inverse[slot_index].astype(jnp.int32)


def draw_lengths(key, part):
    key = jax.random.fold_in(key, 23)
    key_one, key_two = jax.random.split(key)
    devices = BEAMS // BEAM_DEV
    shortened = jax.random.randint(key_one, (devices, BEAM_DEV), 0, 2)
    full_beam = jax.random.randint(key_two, (devices, 1), 0, BEAM_DEV)
    shortened = jnp.where(jnp.arange(BEAM_DEV)[None, :] == full_beam, 0, shortened)
    return ((P_MAX - shortened) * PAGE).reshape(BEAMS).astype(jnp.int32)


def draw_page_table(key, part):
    key = jax.random.fold_in(key, 37)
    devices = BEAMS // BEAM_DEV
    key_list = jax.random.split(key, devices)
    orderings = jax.vmap(lambda single: jax.random.permutation(single, POOL))(key_list)
    return orderings.reshape(BEAMS, P_MAX).astype(jnp.int32)


def draw_queries(key, part):
    key = jax.random.fold_in(key, 51)
    key_one = jax.random.fold_in(key, 0)
    base_draw = jax.random.normal(key_one, (BEAMS, QH, HD), jnp.float32)
    return jnp.clip(base_draw, -6.0, 6.0).astype(jnp.bfloat16)


def shard_levels(rng, shape, shards, low, top_value):
    def one(axis_at, shards_of):
        draws = jax.random.uniform(jax.random.fold_in(jax.random.fold_in(rng, 6), axis_at), (shards_of,), jnp.float32, low / len(shards), top_value / len(shards))
        return jnp.repeat(jnp.exp(draws), shape[axis_at] // shards_of).reshape((-1,) + (1,) * (len(shape) - axis_at - 1))

    level = one(*shards[0])
    for cut in shards[1:]:
        level = level * one(*cut)
    return level


def noise(rng, extent, width, bound, cuts=(), kind=jnp.bfloat16):
    level = shard_levels(rng, extent, cuts, -0.22, 0.18) if cuts else 1.0
    values = jax.random.normal(rng, extent, jnp.float32) * width * level
    return jnp.minimum(jnp.maximum(values, -bound), bound).astype(kind)


def setup_inputs(seed: int = 0, part: int = 0) -> dict:
    streams_of = jax.random.split(jax.random.key(seed), 10)
    part_keys = jax.random.split(jax.random.fold_in(streams_of[9], part), 10)
    return {
        "queries": draw_queries(jax.random.fold_in(jax.random.fold_in(streams_of[9], part), 71), part),
        "new_entries": noise(part_keys[1], (BEAMS, 2, KVH, HD), 1.0, 6.0, ((0, 8), (2, 2))),
        "cache_pages": noise(part_keys[2], (PAGES, 2, KVH, PAGE, HD), 1.0, 6.0, ((0, 8), (2, 2))),
        "cache_scales": jnp.clip(jnp.exp(math.log(2.0) - 1.3862944 * jax.random.uniform(part_keys[3], (PAGES, 2, KVH), jnp.float32) ** shard_levels(part_keys[3], (PAGES, 2, KVH), ((0, 8), (2, 2)), -0.2, 0.2)), 0.5, 2.0).astype(jnp.bfloat16),
        "page_table": draw_page_table(jax.random.fold_in(jax.random.fold_in(streams_of[9], part), 71), part),
        "lengths": draw_lengths(jax.random.fold_in(jax.random.fold_in(streams_of[9], part), 71), part),
        "parent": draw_parent(jax.random.fold_in(jax.random.fold_in(streams_of[9], part), 71), part),
        "placement": draw_placement(jax.random.fold_in(jax.random.fold_in(streams_of[9], part), 71), part),
        "out_weight": noise(streams_of[8], (QH * HD, DOUT), (QH * HD) ** -0.5, 0.125, ((0, 2),)),
    }


def attend_child(query, entries, block, scale_block, length):
    group_size = QH // KVH
    factor = 1.0 / math.sqrt(HD)
    dequant = block.astype(jnp.float32) * scale_block.astype(jnp.float32)[:, :, :, None, None]
    key_rows = jnp.transpose(dequant[:, 0], (1, 0, 2, 3)).reshape(KVH, P_MAX * PAGE, HD)
    value_rows = jnp.transpose(dequant[:, 1], (1, 0, 2, 3)).reshape(KVH, P_MAX * PAGE, HD)
    grouped = query.astype(jnp.float32).reshape(KVH, group_size, HD)
    scores = jnp.einsum('kgd,ktd->kgt', grouped, key_rows) * factor
    visible = jnp.arange(P_MAX * PAGE, dtype=jnp.int32) < length
    scores = jnp.where(visible[None, None, :], scores, -jnp.inf)
    fresh_key = entries[0].astype(jnp.float32)
    fresh_score = jnp.einsum('kgd,kd->kg', grouped, fresh_key) * factor
    highest = jnp.maximum(lax.optimization_barrier(jnp.max(scores, axis=2)), fresh_score)
    weights = jnp.where(visible[None, None, :], jnp.exp(scores - highest[:, :, None]), 0.0)
    fresh_weight = jnp.exp(fresh_score - highest)
    denominator = lax.optimization_barrier(jnp.sum(weights, axis=2)) + fresh_weight
    rounded = lax.optimization_barrier(weights.astype(jnp.bfloat16)).astype(jnp.float32)
    fresh_rounded = lax.optimization_barrier(fresh_weight.astype(jnp.bfloat16)).astype(jnp.float32)
    summed = jnp.einsum('kgt,ktd->kgd', rounded, value_rows)
    summed = summed + fresh_rounded[:, :, None] * entries[1].astype(jnp.float32)[:, None, :]
    return (summed / denominator[:, :, None]).reshape(QH * HD).astype(jnp.bfloat16)

def reference(queries, new_entries, cache_pages, cache_scales, page_table, lengths, parent, placement, out_weight):
    parent_slot = placement[parent]

    def one_child(child_index):
        slot_index = parent_slot[child_index]
        home_device = slot_index // BEAM_DEV
        page_index = (home_device * POOL + page_table[slot_index]).astype(jnp.int32)
        return attend_child(queries[child_index], new_entries[child_index], cache_pages[page_index], cache_scales[page_index], lengths[slot_index])
    attended = lax.map(one_child, jnp.arange(BEAMS, dtype=jnp.int32))
    return jnp.dot(attended, out_weight, preferred_element_type=jnp.float32).astype(jnp.bfloat16)
```

```python
import functools
import math

import jax
import jax.numpy as jnp
from jax import lax
from jax.experimental import pallas as pl
from jax.experimental.pallas import tpu as pltpu
from jax.sharding import PartitionSpec as P

ITEM_ROWS = 16
VMEM = pltpu.VMEM
SMEM = pltpu.SMEM


def pack_kernel(
    beams,
    slots,
    parent_ref,
    placement_ref,
    query_ref,
    entry_ref,
    scale_ref,
    send_ref,
    select_ref,
    scale_out_ref,
    count_ref,
):
    heads, children, head_size = query_ref.shape
    entry_rows = entry_ref.shape[0]
    per_child = entry_rows // children
    own = lax.axis_index("beam")
    scale_out_ref[...] = scale_ref[...].astype(jnp.float32)
    for index in range(beams):
        count_ref[index] = 0
    query_lane = lax.broadcasted_iota(jnp.int32, (8, heads * children), 1)
    entry_lane = lax.broadcasted_iota(jnp.int32, (8, entry_rows), 1)
    query_child = query_lane % children
    entry_child = entry_lane // per_child
    query_row = query_lane // children
    entry_row = entry_lane % per_child + heads
    select_shape = select_ref.shape
    child_row = lax.broadcasted_iota(jnp.int32, select_shape, 0)
    select_lane = lax.broadcasted_iota(jnp.int32, select_shape, 1)
    select_item = (select_lane // (2 * slots)) * slots + select_lane % slots
    select = jnp.zeros(select_shape, jnp.int32)
    for child in range(children):
        slot = placement_ref[parent_ref[own * children + child]]
        source = slot // children
        rank = count_ref[source]
        count_ref[source] = rank + 1
        item = source * slots + rank
        query_row = jnp.where(query_child == child, query_row + item * ITEM_ROWS, query_row)
        entry_row = jnp.where(entry_child == child, entry_row + item * ITEM_ROWS, entry_row)
        select = jnp.where((child_row == child) & (select_item == item), 1, select)
    select_ref[...] = select.astype(jnp.float32).astype(jnp.bfloat16)
    rows = beams * slots * ITEM_ROWS
    row_of = lax.broadcasted_iota(jnp.int32, (rows, heads * children), 0)
    pick = (row_of == query_row[:1]).astype(jnp.float32).astype(jnp.bfloat16)
    entry_row_of = lax.broadcasted_iota(jnp.int32, (rows, entry_rows), 0)
    entry_pick = (entry_row_of == entry_row[:1]).astype(jnp.float32).astype(jnp.bfloat16)
    moved = jnp.dot(
        pick, query_ref[...].reshape(heads * children, head_size), preferred_element_type=jnp.float32
    )
    moved += jnp.dot(entry_pick, entry_ref[...], preferred_element_type=jnp.float32)
    send_ref[...] = moved.astype(jnp.bfloat16).reshape(send_ref.shape)


def route_kernel(
    beams,
    slots,
    children,
    parent_ref,
    placement_ref,
    table_ref,
    length_ref,
    page_ref,
    item_length_ref,
):
    own = lax.axis_index("beam")
    page_limit = table_ref.shape[0]

    def clear(item, _):
        item_length_ref[item] = length_ref[own * children]
        for page in range(page_limit):
            page_ref[item * page_limit + page] = table_ref[page, 0]
        return 0

    lax.fori_loop(0, beams * slots, clear, 0)

    def one_index(index, _):
        def one_child(child, rank):
            slot = placement_ref[parent_ref[index * children + child]]
            mine = slot // children == own

            @pl.when(mine)
            def _():
                item = index * slots + rank
                item_length_ref[item] = length_ref[slot]
                for page in range(page_limit):
                    page_ref[item * page_limit + page] = table_ref[page, slot % children]

            return rank + mine.astype(jnp.int32)

        lax.fori_loop(0, children, one_child, 0, unroll=4)
        return 0

    lax.fori_loop(0, beams, one_index, 0)


def attend_kernel(
    slots,
    factor,
    page_ref,
    item_length_ref,
    scale_ref,
    arrived_ref,
    pages_ref,
    weight_ref,
    out_ref,
    attended_ref,
):
    item_count = arrived_ref.shape[0]
    page_count, _, key_heads, page_rows, head_size = pages_ref.shape
    page_limit = page_ref.shape[0] // item_count
    heads = weight_ref.shape[0] // head_size
    group = heads // key_heads
    row = lax.broadcasted_iota(jnp.int32, (ITEM_ROWS, head_size), 0)
    row_head = [(row >= head * group) & (row < (head + 1) * group) for head in range(key_heads)]
    column = row[:, :1]
    column_head = [(column >= head * group) & (column < (head + 1) * group) for head in range(key_heads)]

    def by_head(masks, parts):
        result = jnp.zeros((), jnp.float32)
        for mask, part in zip(masks, parts):
            result = jnp.where(mask, part, result)
        return result

    for item in range(item_count):
        packed = arrived_ref[item].astype(jnp.float32)
        wide = jnp.concatenate([jnp.where(mask, packed, 0.0) for mask in row_head], axis=1).astype(jnp.bfloat16)
        length = item_length_ref[item]
        numbers = [page_ref[item * page_limit + page] for page in range(page_limit)]
        scores = []
        for page, number in enumerate(numbers):
            keys = jnp.concatenate([pages_ref[number, 0, head] for head in range(key_heads)], axis=1)
            raw = lax.dot_general(wide, keys, (((1,), (1,)), ((), ())), preferred_element_type=jnp.float32)
            key_scale = by_head(column_head, [scale_ref[head, number] * factor for head in range(key_heads)])
            hidden = jnp.where(page * page_rows < length, 0.0, -jnp.inf)
            scores.append(raw * key_scale + hidden)
        fresh_key = by_head(row_head, [packed[heads + head][None] for head in range(key_heads)])
        fresh_value = by_head(row_head, [packed[heads + key_heads + head][None] for head in range(key_heads)])
        fresh = jnp.sum(packed * fresh_key, axis=1, keepdims=True) * factor
        highest = jnp.maximum(jnp.max(functools.reduce(jnp.maximum, scores), axis=1, keepdims=True), fresh)
        fresh_weight = jnp.exp(fresh - highest)
        total = jnp.zeros((), jnp.float32)
        summed = fresh_weight.astype(jnp.bfloat16).astype(jnp.float32) * fresh_value
        for number, score in zip(numbers, scores):
            weights = jnp.exp(score - highest)
            total = total + weights
            values = jnp.concatenate([pages_ref[number, 1, head] for head in range(key_heads)], axis=1)
            product = jnp.dot(weights.astype(jnp.bfloat16), values, preferred_element_type=jnp.float32)
            summed = summed + by_head(
                row_head,
                [
                    product[:, head * head_size : (head + 1) * head_size] * scale_ref[key_heads + head, number]
                    for head in range(key_heads)
                ],
            )
        denominator = jnp.sum(total, axis=1, keepdims=True) + fresh_weight
        attended_ref[item * ITEM_ROWS : (item + 1) * ITEM_ROWS, :] = summed / denominator
    attended = jnp.concatenate(
        [attended_ref[pl.ds(head, item_count, stride=ITEM_ROWS), :] for head in range(heads)], axis=1
    ).astype(jnp.bfloat16)
    width = out_ref.shape[2]
    for half in range(2):
        part = jnp.dot(
            attended, weight_ref[:, half * width : (half + 1) * width], preferred_element_type=jnp.float32
        ).astype(jnp.bfloat16)
        for index in range(item_count // slots):
            out_ref[index * 2 + half] = part[index * slots : (index + 1) * slots]


def finish_kernel(select_ref, arrived_ref, out_ref):
    members, slots, width = arrived_ref.shape
    parts = arrived_ref[...].reshape(members * slots, width)
    out_ref[...] = jnp.dot(select_ref[...], parts, preferred_element_type=jnp.float32).astype(out_ref.dtype)


def spec(space):
    return pl.BlockSpec(memory_space=space)


def on_device(
    queries,
    new_entries,
    cache_pages,
    cache_scales,
    page_table,
    lengths,
    parent,
    placement,
    out_weight,
):
    beams = lax.axis_size("beam")
    children, heads, head_size = queries.shape
    key_heads = new_entries.shape[2]
    page_limit = page_table.shape[1]
    page_count = cache_pages.shape[0]
    wanted = (children + beams - 1) // beams
    slots = wanted + wanted % 2
    items = beams * slots
    width = out_weight.shape[1] // 2
    limit = 16 * 1024 * 1024
    params = pltpu.CompilerParams(vmem_limit_bytes=limit)

    query_rows = jnp.transpose(queries, (1, 0, 2))
    entry_rows = new_entries.reshape(children * 2 * key_heads, head_size)
    scales = jnp.transpose(cache_scales, (1, 2, 0)).reshape(2 * key_heads, page_count)

    send, select, scale_values = pl.pallas_call(
        functools.partial(pack_kernel, beams, slots),
        out_shape=(
            jax.ShapeDtypeStruct((beams, slots * ITEM_ROWS, head_size), jnp.bfloat16),
            jax.ShapeDtypeStruct((children, 2 * items), jnp.bfloat16),
            jax.ShapeDtypeStruct((2 * key_heads, page_count), jnp.float32),
        ),
        in_specs=[spec(SMEM)] * 2 + [spec(VMEM)] * 3,
        out_specs=(spec(VMEM),) * 3,
        scratch_shapes=[SMEM((beams,), jnp.int32)],
        compiler_params=params,
        name="pack",
    )(parent, placement, query_rows, entry_rows, scales)

    arrived = lax.all_to_all(send, "beam", split_axis=0, concat_axis=0, tiled=True)

    item_pages, item_lengths = pl.pallas_call(
        functools.partial(route_kernel, beams, slots, children),
        out_shape=(
            jax.ShapeDtypeStruct((items * page_limit,), jnp.int32),
            jax.ShapeDtypeStruct((items,), jnp.int32),
        ),
        in_specs=[spec(SMEM)] * 4,
        out_specs=(spec(SMEM),) * 2,
        compiler_params=params,
        name="route",
    )(parent, placement, jnp.transpose(page_table), lengths)

    partial_sums = pl.pallas_call(
        functools.partial(attend_kernel, slots, 1.0 / math.sqrt(head_size)),
        out_shape=jax.ShapeDtypeStruct((beams * 2, slots, width), jnp.bfloat16),
        in_specs=[spec(SMEM)] * 3 + [spec(VMEM)] * 3,
        out_specs=spec(VMEM),
        scratch_shapes=[VMEM((items * ITEM_ROWS, head_size), jnp.float32)],
        compiler_params=pltpu.CompilerParams(vmem_limit_bytes=limit),
        name="attend",
    )(
        item_pages,
        item_lengths,
        scale_values,
        arrived.reshape(items, ITEM_ROWS, head_size),
        pltpu.with_memory_space_constraint(cache_pages, VMEM),
        pltpu.with_memory_space_constraint(out_weight, VMEM),
    )

    returned = lax.all_to_all(partial_sums, ("beam", "tp"), split_axis=0, concat_axis=0, tiled=True)

    return pl.pallas_call(
        finish_kernel,
        out_shape=jax.ShapeDtypeStruct((children, width), jnp.bfloat16),
        in_specs=[spec(VMEM)] * 2,
        out_specs=spec(VMEM),
        compiler_params=params,
        name="finish",
    )(select, returned)


def solution(mesh):
    return jax.shard_map(
        on_device,
        mesh=mesh,
        in_specs=(
            P(("grp", "beam"), "tp", None),
            P(("grp", "beam"), None, "tp", None),
            P(("grp", "beam"), None, "tp", None, None),
            P(("grp", "beam"), None, "tp"),
            P(("grp", "beam"), None),
            P("grp"),
            P("grp"),
            P("grp"),
            P("tp", None),
        ),
        out_specs=P(("grp", "beam"), "tp"),
        check_vma=False,
    )
```

```python
import functools
import math

import jax
import jax.numpy as jnp
from jax import lax
from jax.experimental import pallas as pl
from jax.experimental.pallas import tpu as pltpu
from jax.sharding import PartitionSpec as P

ITEM_ROWS = 16
VMEM = pltpu.VMEM
SMEM = pltpu.SMEM
HBM = pltpu.HBM


def fetch(pairs, sem_ref):
    copies = [pltpu.make_async_copy(a, b, sem_ref.at[i]) for i, (a, b) in enumerate(pairs)]
    for copy in copies:
        copy.start()
    return copies


def pack_kernel(
    beams,
    slots,
    used,
    parent_hbm,
    placement_hbm,
    query_hbm,
    entry_hbm,
    table_hbm,
    length_hbm,
    send_hbm,
    page_ref,
    item_length_ref,
    own_item_ref,
    parent_ref,
    placement_ref,
    query_ref,
    entry_ref,
    table_ref,
    length_ref,
    send_ref,
    item_ref,
    count_ref,
    sem_ref,
):
    heads, children, head_size = query_ref.shape
    entry_rows = entry_ref.shape[0]
    per_child = entry_rows // children
    page_limit = table_ref.shape[0]
    copies = fetch(
        [
            (parent_hbm, parent_ref),
            (placement_hbm, placement_ref),
            (query_hbm, query_ref),
            (entry_hbm, entry_ref),
            (table_hbm, table_ref),
            (length_hbm, length_ref),
        ],
        sem_ref,
    )
    own = lax.axis_index("beam")
    for index in range(beams):
        count_ref[index] = 0
    query_lane = lax.broadcasted_iota(jnp.int32, (8, heads * children), 1)
    entry_lane = lax.broadcasted_iota(jnp.int32, (8, entry_rows), 1)
    query_child = query_lane % children
    entry_child = entry_lane // per_child
    query_row = query_lane // children
    entry_row = entry_lane % per_child + heads
    copies[0].wait()
    copies[1].wait()
    own_slots = [placement_ref[parent_ref[own * children + child]] for child in range(children)]
    for child, slot in enumerate(own_slots):
        source = slot // children
        rank = count_ref[source]
        count_ref[source] = rank + 1
        item = source * slots + rank
        own_item_ref[child] = item
        first = item * ITEM_ROWS
        query_row = jnp.where(query_child == child, query_row + first, query_row)
        entry_row = jnp.where(entry_child == child, entry_row + first, entry_row)
    rows = beams * slots * ITEM_ROWS
    row_of = lax.broadcasted_iota(jnp.int32, (rows, heads * children), 0)
    pick = (row_of == query_row[:1]).astype(jnp.float32).astype(jnp.bfloat16)
    entry_row_of = lax.broadcasted_iota(jnp.int32, (rows, entry_rows), 0)
    entry_pick = (entry_row_of == entry_row[:1]).astype(jnp.float32).astype(jnp.bfloat16)
    copies[2].wait()
    copies[3].wait()
    moved = jnp.dot(
        pick, query_ref[...].reshape(heads * children, head_size), preferred_element_type=jnp.float32
    )
    moved += jnp.dot(entry_pick, entry_ref[...], preferred_element_type=jnp.float32)
    send_ref[...] = moved.astype(jnp.bfloat16).reshape(send_ref.shape)
    send_copy = pltpu.make_async_copy(send_ref, send_hbm, sem_ref.at[6])
    send_copy.start()

    def one_index(index, _):
        asked = [placement_ref[parent_ref[index * children + child]] for child in range(children)]
        place = index * slots
        for slot in asked:
            item_ref[place] = slot % children
            place = place + (slot // children == own).astype(jnp.int32)
        return 0

    lax.fori_loop(0, beams, one_index, 0)
    copies[4].wait()
    copies[5].wait()
    for place, item in enumerate(used):
        local = item_ref[item]
        item_length_ref[place] = length_ref[own * children + local]
        for page in range(page_limit):
            page_ref[place * page_limit + page] = table_ref[page, local]
    send_copy.wait()


def bring_kernel(
    slots,
    page_ref,
    own_item_ref,
    scale_hbm,
    pages_hbm,
    scale_ref,
    select_ref,
    early_ref,
    scale_in_ref,
    scale_wide_ref,
    scale_sem_ref,
    page_sem_ref,
):
    scale_copy = pltpu.make_async_copy(scale_hbm, scale_in_ref, scale_sem_ref.at[0])
    scale_copy.start()
    page_copies = fetch(
        [(pages_hbm.at[page_ref[at]], early_ref.at[at]) for at in range(early_ref.shape[0])], page_sem_ref
    )
    select_shape = select_ref.shape
    child_row = lax.broadcasted_iota(jnp.int32, select_shape, 0)
    select_lane = lax.broadcasted_iota(jnp.int32, select_shape, 1)
    select_item = (select_lane // (2 * slots)) * slots + select_lane % slots
    wanted = jnp.zeros(select_shape, jnp.int32)
    for child in range(select_shape[0]):
        wanted = jnp.where(child_row == child, own_item_ref[child], wanted)
    select_ref[...] = (select_item == wanted).astype(jnp.float32).astype(jnp.bfloat16)
    scale_copy.wait()
    scale_wide_ref[...] = scale_in_ref[...].astype(jnp.float32)
    wide_copy = pltpu.make_async_copy(scale_wide_ref, scale_ref, scale_sem_ref.at[1])
    wide_copy.start()
    wide_copy.wait()
    for copy in page_copies:
        copy.wait()


def attend_kernel(
    slots,
    used,
    factor,
    page_ref,
    item_length_ref,
    scale_ref,
    arrived_ref,
    early_ref,
    pages_hbm,
    weight_hbm,
    out_ref,
    late_ref,
    weight_ref,
    score_ref,
    rounded_ref,
    denominator_ref,
    attended_ref,
    page_sem_ref,
    weight_sem_ref,
):
    item_count = arrived_ref.shape[0]
    early = early_ref.shape[0]
    _, _, key_heads, page_rows, head_size = early_ref.shape
    page_limit = page_ref.shape[0] // len(used)
    heads = weight_ref.shape[0] // head_size
    group = heads // key_heads
    late_copies = fetch(
        [(pages_hbm.at[page_ref[early + late]], late_ref.at[late]) for late in range(late_ref.shape[0])], page_sem_ref
    )
    cuts = [0] + [heads * part // 5 * head_size for part in (3, 4, 5)]
    weight_rows = [pl.ds(low, high - low) for low, high in zip(cuts, cuts[1:])]
    row = lax.broadcasted_iota(jnp.int32, (ITEM_ROWS, head_size), 0)
    row_head = [(row >= head * group) & (row < (head + 1) * group) for head in range(key_heads)]

    def by_head(parts):
        result = jnp.zeros((ITEM_ROWS, head_size), jnp.float32)
        for mask, part in zip(row_head, parts):
            result = jnp.where(mask, part, result)
        return result

    def rows_of(item):
        return slice(item * ITEM_ROWS, (item + 1) * ITEM_ROWS)

    def both_heads(place, page, which):
        at = place * page_limit + page
        ref, at = (early_ref, at) if at < early else (late_ref, at - early)
        return jnp.concatenate([ref[at, which, head] for head in range(key_heads)], axis=1)

    def scores_of(place, item):
        packed = arrived_ref[item].astype(jnp.float32)
        wide = jnp.concatenate([jnp.where(mask, packed, 0.0) for mask in row_head], axis=1).astype(jnp.bfloat16)
        length = item_length_ref[place]
        for page in range(page_limit):
            number = page_ref[place * page_limit + page]
            raw = lax.dot_general(
                wide, both_heads(place, page, 0), (((1,), (1,)), ((), ())), preferred_element_type=jnp.float32
            )
            key_scale = by_head([scale_ref[head, number] * factor for head in range(key_heads)])
            hidden = jnp.where(page * page_rows < length, 0.0, -jnp.inf)
            score_ref[rows_of(place), page * page_rows : (page + 1) * page_rows] = raw * key_scale + hidden

    def weights_of(place, item):
        packed = arrived_ref[item].astype(jnp.float32)
        fresh_key = by_head([packed[heads + head][None] for head in range(key_heads)])
        fresh_value = by_head([packed[heads + key_heads + head][None] for head in range(key_heads)])
        scores = score_ref[rows_of(place), :]
        fresh = jnp.sum(packed * fresh_key, axis=1, keepdims=True) * factor
        highest = jnp.maximum(jnp.max(scores, axis=1, keepdims=True), fresh)
        fresh_weight = jnp.exp(fresh - highest)
        weights = jnp.exp(scores - highest)
        rounded_ref[rows_of(place), :] = weights.astype(jnp.bfloat16)
        denominator = jnp.sum(weights, axis=1, keepdims=True) + fresh_weight
        denominator_ref[rows_of(place), :] = jnp.broadcast_to(denominator, (ITEM_ROWS, head_size))
        attended_ref[rows_of(item), :] = fresh_weight.astype(jnp.bfloat16).astype(jnp.float32) * fresh_value

    def values_of(place, item):
        summed = attended_ref[rows_of(item), :]
        for page in range(page_limit):
            number = page_ref[place * page_limit + page]
            product = jnp.dot(
                rounded_ref[rows_of(place), page * page_rows : (page + 1) * page_rows],
                both_heads(place, page, 1),
                preferred_element_type=jnp.float32,
            )
            summed = summed + by_head(
                [
                    product[:, head * head_size : (head + 1) * head_size] * scale_ref[key_heads + head, number]
                    for head in range(key_heads)
                ],
            )
        attended_ref[rows_of(item), :] = summed / denominator_ref[rows_of(place), :]

    if len(used) < item_count:
        attended_ref[...] = jnp.zeros_like(attended_ref)
    places = list(enumerate(used))
    late_places = places[early // page_limit :]
    share = len(late_places) // 4
    groups = [places[: early // page_limit]]
    groups += [late_places[low : low + share] for low in range(0, len(late_places), share)]
    for number, group_of in enumerate(groups):
        if number > 0:
            for copy in late_copies[(number - 1) * share * page_limit : number * share * page_limit]:
                copy.wait()
        if number == 1:
            weight_copies = fetch([(weight_hbm.at[rows], weight_ref.at[rows]) for rows in weight_rows], weight_sem_ref)
        for step in (scores_of, weights_of, values_of):
            for place, item in group_of:
                step(place, item)
    attended = jnp.concatenate(
        [attended_ref[pl.ds(head, item_count, stride=ITEM_ROWS), :] for head in range(heads)], axis=1
    ).astype(jnp.bfloat16)
    total = None
    for copy, low, high in zip(weight_copies, cuts, cuts[1:]):
        copy.wait()
        term = jnp.dot(attended[:, low:high], weight_ref[low:high, :], preferred_element_type=jnp.float32)
        total = term if total is None else total + term
    total = total.astype(jnp.bfloat16)
    width = out_ref.shape[2]
    for half in range(2):
        for index in range(item_count // slots):
            out_ref[index * 2 + half] = total[index * slots : (index + 1) * slots, half * width : (half + 1) * width]


def finish_kernel(select_ref, arrived_ref, out_ref):
    members, slots, width = arrived_ref.shape
    parts = arrived_ref[...].reshape(members * slots, width)
    out_ref[...] = jnp.dot(select_ref[...], parts, preferred_element_type=jnp.float32).astype(out_ref.dtype)


def kept(space, *arrays):
    return tuple(pltpu.with_memory_space_constraint(array, space) for array in arrays)


def spec(space):
    return pl.BlockSpec(memory_space=space)


def on_device(
    queries,
    new_entries,
    cache_pages,
    cache_scales,
    page_table,
    lengths,
    parent,
    placement,
    out_weight,
):
    beams = lax.axis_size("beam")
    children, heads, head_size = queries.shape
    key_heads = new_entries.shape[2]
    page_limit = page_table.shape[1]
    page_count = cache_pages.shape[0]
    page_rows = cache_pages.shape[3]
    wanted = (children + beams - 1) // beams
    slots = wanted + wanted % 2
    items = beams * slots
    used = [index * slots + rank for index in range(beams) for rank in range(wanted)]
    page_total = len(used) * page_limit
    early = min(len(used), 8) * page_limit
    page_shape = cache_pages.shape[1:]
    width = out_weight.shape[1] // 2
    limit = 32 * 1024 * 1024
    params = pltpu.CompilerParams(vmem_limit_bytes=limit)

    query_rows = jnp.transpose(queries, (1, 0, 2))
    entry_rows = new_entries.reshape(children * 2 * key_heads, head_size)
    scales = jnp.transpose(cache_scales, (1, 2, 0)).reshape(2 * key_heads, page_count)

    send, item_pages, item_lengths, own_items = pl.pallas_call(
        functools.partial(pack_kernel, beams, slots, used),
        out_shape=(
            HBM((beams, slots * ITEM_ROWS, head_size), jnp.bfloat16),
            SMEM((page_total,), jnp.int32),
            SMEM((len(used),), jnp.int32),
            SMEM((children,), jnp.int32),
        ),
        in_specs=[spec(HBM)] * 6,
        out_specs=(spec(HBM),) + (spec(SMEM),) * 3,
        scratch_shapes=[
            SMEM(parent.shape, jnp.int32),
            SMEM(placement.shape, jnp.int32),
            VMEM(query_rows.shape, jnp.bfloat16),
            VMEM(entry_rows.shape, jnp.bfloat16),
            SMEM(page_table.shape[::-1], jnp.int32),
            SMEM(lengths.shape, jnp.int32),
            VMEM((beams, slots * ITEM_ROWS, head_size), jnp.bfloat16),
            SMEM((items + 1,), jnp.int32),
            SMEM((beams,), jnp.int32),
            pltpu.SemaphoreType.DMA((7,)),
        ],
        compiler_params=params,
        name="pack",
    )(*kept(HBM, parent, placement, query_rows, entry_rows, jnp.transpose(page_table), lengths))

    arrived = lax.all_to_all(send, "beam", split_axis=0, concat_axis=0, tiled=True)

    scale_values, select, early_pages = pl.pallas_call(
        functools.partial(bring_kernel, slots),
        out_shape=(
            SMEM(scales.shape, jnp.float32),
            VMEM((children, 2 * items), jnp.bfloat16),
            VMEM((early,) + page_shape, jnp.bfloat16),
        ),
        in_specs=[spec(SMEM)] * 2 + [spec(HBM)] * 2,
        out_specs=(spec(SMEM), spec(VMEM), spec(VMEM)),
        scratch_shapes=[
            VMEM(scales.shape, jnp.bfloat16),
            VMEM(scales.shape, jnp.float32),
            pltpu.SemaphoreType.DMA((2,)),
            pltpu.SemaphoreType.DMA((early,)),
        ],
        compiler_params=params,
        name="bring",
    )(*kept(SMEM, item_pages, own_items), *kept(HBM, scales, cache_pages))

    partial_sums = pl.pallas_call(
        functools.partial(attend_kernel, slots, used, 1.0 / math.sqrt(head_size)),
        out_shape=jax.ShapeDtypeStruct((beams * 2, slots, width), jnp.bfloat16),
        in_specs=[spec(SMEM)] * 3 + [spec(VMEM)] * 2 + [spec(HBM)] * 2,
        out_specs=spec(VMEM),
        scratch_shapes=[
            VMEM((page_total - early,) + page_shape, jnp.bfloat16),
            VMEM(out_weight.shape, jnp.bfloat16),
            VMEM((len(used) * ITEM_ROWS, page_limit * page_rows), jnp.float32),
            VMEM((len(used) * ITEM_ROWS, page_limit * page_rows), jnp.bfloat16),
            VMEM((len(used) * ITEM_ROWS, head_size), jnp.float32),
            VMEM((items * ITEM_ROWS, head_size), jnp.float32),
            pltpu.SemaphoreType.DMA((page_total - early,)),
            pltpu.SemaphoreType.DMA((3,)),
        ],
        compiler_params=params,
        name="attend",
    )(
        *kept(SMEM, item_pages, item_lengths, scale_values),
        *kept(VMEM, arrived.reshape(items, ITEM_ROWS, head_size), early_pages),
        *kept(HBM, cache_pages, out_weight),
    )

    returned = lax.all_to_all(partial_sums, ("beam", "tp"), split_axis=0, concat_axis=0, tiled=True)

    return pl.pallas_call(
        finish_kernel,
        out_shape=jax.ShapeDtypeStruct((children, width), jnp.bfloat16),
        in_specs=[spec(VMEM)] * 2,
        out_specs=spec(VMEM),
        compiler_params=params,
        name="finish",
    )(*kept(VMEM, select, returned))


def solution(mesh):
    return jax.shard_map(
        on_device,
        mesh=mesh,
        in_specs=(
            P(("grp", "beam"), "tp", None),
            P(("grp", "beam"), None, "tp", None),
            P(("grp", "beam"), None, "tp", None, None),
            P(("grp", "beam"), None, "tp"),
            P(("grp", "beam"), None),
            P("grp"),
            P("grp"),
            P("grp"),
            P("tp", None),
        ),
        out_specs=P(("grp", "beam"), "tp"),
        check_vma=False,
    )
```

```python
import functools
import math

import jax
import jax.numpy as jnp
from jax import lax
from jax.experimental import pallas as pl
from jax.experimental.pallas import tpu as pltpu
from jax.sharding import PartitionSpec as P

ITEM_ROWS = 16
VMEM = pltpu.VMEM
SMEM = pltpu.SMEM
HBM = pltpu.HBM


def fetch(pairs, sem_ref):
    copies = [pltpu.make_async_copy(a, b, sem_ref.at[i]) for i, (a, b) in enumerate(pairs)]
    for copy in copies:
        copy.start()
    return copies


def pack_kernel(
    beams,
    slots,
    used,
    parent_hbm,
    placement_hbm,
    query_hbm,
    entry_hbm,
    table_hbm,
    length_hbm,
    scale_hbm,
    pages_hbm,
    weight_hbm,
    send_ref,
    page_ref,
    item_length_ref,
    scale_ref,
    select_ref,
    pages_ref,
    weight_ref,
    parent_ref,
    placement_ref,
    query_ref,
    entry_ref,
    table_ref,
    length_ref,
    scale_in_ref,
    scale_wide_ref,
    item_ref,
    count_ref,
    sem_ref,
):
    heads, children, head_size = query_ref.shape
    entry_rows = entry_ref.shape[0]
    per_child = entry_rows // children
    page_limit = table_ref.shape[0]
    copies = fetch(
        [
            (parent_hbm, parent_ref),
            (placement_hbm, placement_ref),
            (query_hbm, query_ref),
            (entry_hbm, entry_ref),
            (table_hbm, table_ref),
            (length_hbm, length_ref),
            (scale_hbm, scale_in_ref),
            (pages_hbm, pages_ref),
            (weight_hbm.at[pl.ds(0, weight_ref.shape[0])], weight_ref),
        ],
        sem_ref,
    )
    own = lax.axis_index("beam")
    for index in range(beams):
        count_ref[index] = 0
    query_lane = lax.broadcasted_iota(jnp.int32, (8, heads * children), 1)
    entry_lane = lax.broadcasted_iota(jnp.int32, (8, entry_rows), 1)
    query_child = query_lane % children
    entry_child = entry_lane // per_child
    query_row = query_lane // children
    entry_row = entry_lane % per_child + heads
    select_shape = select_ref.shape
    child_row = lax.broadcasted_iota(jnp.int32, select_shape, 0)
    select_lane = lax.broadcasted_iota(jnp.int32, select_shape, 1)
    select_item = (select_lane // (2 * slots)) * slots + select_lane % slots
    wanted = jnp.zeros(select_shape, jnp.int32)
    copies[0].wait()
    copies[1].wait()
    own_slots = [placement_ref[parent_ref[own * children + child]] for child in range(children)]
    for child, slot in enumerate(own_slots):
        source = slot // children
        rank = count_ref[source]
        count_ref[source] = rank + 1
        item = source * slots + rank
        wanted = jnp.where(child_row == child, item, wanted)
        first = item * ITEM_ROWS
        query_row = jnp.where(query_child == child, query_row + first, query_row)
        entry_row = jnp.where(entry_child == child, entry_row + first, entry_row)
    rows = beams * slots * ITEM_ROWS
    row_of = lax.broadcasted_iota(jnp.int32, (rows, heads * children), 0)
    pick = (row_of == query_row[:1]).astype(jnp.float32).astype(jnp.bfloat16)
    entry_row_of = lax.broadcasted_iota(jnp.int32, (rows, entry_rows), 0)
    entry_pick = (entry_row_of == entry_row[:1]).astype(jnp.float32).astype(jnp.bfloat16)
    copies[2].wait()
    copies[3].wait()
    moved = jnp.dot(
        pick, query_ref[...].reshape(heads * children, head_size), preferred_element_type=jnp.float32
    )
    moved += jnp.dot(entry_pick, entry_ref[...], preferred_element_type=jnp.float32)
    send_ref[...] = moved.astype(jnp.bfloat16).reshape(send_ref.shape)
    select_ref[...] = (select_item == wanted).astype(jnp.float32).astype(jnp.bfloat16)
    copies[6].wait()
    scale_wide_ref[...] = scale_in_ref[...].astype(jnp.float32)
    scale_copy = pltpu.make_async_copy(scale_wide_ref, scale_ref, sem_ref.at[9])
    scale_copy.start()

    def one_index(index, _):
        asked = [placement_ref[parent_ref[index * children + child]] for child in range(children)]
        place = index * slots
        for slot in asked:
            item_ref[place] = slot % children
            place = place + (slot // children == own).astype(jnp.int32)
        return 0

    lax.fori_loop(0, beams, one_index, 0)
    copies[4].wait()
    copies[5].wait()
    for place, item in enumerate(used):
        local = item_ref[item]
        item_length_ref[place] = length_ref[own * children + local]
        for page in range(page_limit):
            page_ref[place * page_limit + page] = table_ref[page, local]
    scale_copy.wait()
    copies[7].wait()
    copies[8].wait()


def attend_kernel(
    slots,
    used,
    factor,
    page_ref,
    item_length_ref,
    scale_ref,
    arrived_ref,
    pages_ref,
    weight_ref,
    weight_hbm,
    out_ref,
    weight_tail_ref,
    score_ref,
    rounded_ref,
    denominator_ref,
    attended_ref,
    sem_ref,
):
    item_count = arrived_ref.shape[0]
    _, _, key_heads, page_rows, head_size = pages_ref.shape
    page_limit = page_ref.shape[0] // len(used)
    cut, tail = weight_ref.shape[0], 0
    heads = (cut + tail) // head_size
    group = heads // key_heads
    row = lax.broadcasted_iota(jnp.int32, (ITEM_ROWS, head_size), 0)
    row_head = [(row >= head * group) & (row < (head + 1) * group) for head in range(key_heads)]

    def by_head(parts):
        result = jnp.zeros((ITEM_ROWS, head_size), jnp.float32)
        for mask, part in zip(row_head, parts):
            result = jnp.where(mask, part, result)
        return result

    def rows_of(item):
        return slice(item * ITEM_ROWS, (item + 1) * ITEM_ROWS)

    def both_heads(number, which):
        return jnp.concatenate([pages_ref[number, which, head] for head in range(key_heads)], axis=1)

    def scores_of(place, item):
        packed = arrived_ref[item].astype(jnp.float32)
        wide = jnp.concatenate([jnp.where(mask, packed, 0.0) for mask in row_head], axis=1).astype(jnp.bfloat16)
        length = item_length_ref[place]
        for page in range(page_limit):
            number = page_ref[place * page_limit + page]
            raw = lax.dot_general(
                wide, both_heads(number, 0), (((1,), (1,)), ((), ())), preferred_element_type=jnp.float32
            )
            key_scale = by_head([scale_ref[head, number] * factor for head in range(key_heads)])
            hidden = jnp.where(page * page_rows < length, 0.0, -jnp.inf)
            score_ref[rows_of(place), page * page_rows : (page + 1) * page_rows] = raw * key_scale + hidden

    def weights_of(place, item):
        packed = arrived_ref[item].astype(jnp.float32)
        fresh_key = by_head([packed[heads + head][None] for head in range(key_heads)])
        fresh_value = by_head([packed[heads + key_heads + head][None] for head in range(key_heads)])
        scores = score_ref[rows_of(place), :]
        fresh = jnp.sum(packed * fresh_key, axis=1, keepdims=True) * factor
        highest = jnp.maximum(jnp.max(scores, axis=1, keepdims=True), fresh)
        fresh_weight = jnp.exp(fresh - highest)
        weights = jnp.exp(scores - highest)
        rounded_ref[rows_of(place), :] = weights.astype(jnp.bfloat16)
        denominator = jnp.sum(weights, axis=1, keepdims=True) + fresh_weight
        denominator_ref[rows_of(place), :] = jnp.broadcast_to(denominator, (ITEM_ROWS, head_size))
        attended_ref[rows_of(item), :] = fresh_weight.astype(jnp.bfloat16).astype(jnp.float32) * fresh_value

    def values_of(place, item):
        summed = attended_ref[rows_of(item), :]
        for page in range(page_limit):
            number = page_ref[place * page_limit + page]
            product = jnp.dot(
                rounded_ref[rows_of(place), page * page_rows : (page + 1) * page_rows],
                both_heads(number, 1),
                preferred_element_type=jnp.float32,
            )
            summed = summed + by_head(
                [
                    product[:, head * head_size : (head + 1) * head_size] * scale_ref[key_heads + head, number]
                    for head in range(key_heads)
                ],
            )
        attended_ref[rows_of(item), :] = summed / denominator_ref[rows_of(place), :]

    if len(used) < item_count:
        attended_ref[...] = jnp.zeros_like(attended_ref)
    for step in (scores_of, weights_of, values_of):
        for place, item in enumerate(used):
            step(place, item)
    attended = jnp.concatenate(
        [attended_ref[pl.ds(head, item_count, stride=ITEM_ROWS), :] for head in range(heads)], axis=1
    ).astype(jnp.bfloat16)
    total = jnp.dot(attended[:, :cut], weight_ref[...], preferred_element_type=jnp.float32)
    total = total.astype(jnp.bfloat16)
    width = out_ref.shape[2]
    for half in range(2):
        for index in range(item_count // slots):
            out_ref[index * 2 + half] = total[index * slots : (index + 1) * slots, half * width : (half + 1) * width]


def finish_kernel(select_ref, arrived_ref, out_ref):
    members, slots, width = arrived_ref.shape
    parts = arrived_ref[...].reshape(members * slots, width)
    out_ref[...] = jnp.dot(select_ref[...], parts, preferred_element_type=jnp.float32).astype(out_ref.dtype)


def kept(space, *arrays):
    return tuple(pltpu.with_memory_space_constraint(array, space) for array in arrays)


def spec(space):
    return pl.BlockSpec(memory_space=space)


def on_device(
    queries,
    new_entries,
    cache_pages,
    cache_scales,
    page_table,
    lengths,
    parent,
    placement,
    out_weight,
):
    beams = lax.axis_size("beam")
    children, heads, head_size = queries.shape
    key_heads = new_entries.shape[2]
    page_limit = page_table.shape[1]
    page_count = cache_pages.shape[0]
    page_rows = cache_pages.shape[3]
    wanted = (children + beams - 1) // beams
    slots = wanted + wanted % 2
    items = beams * slots
    used = [index * slots + rank for index in range(beams) for rank in range(wanted)]
    page_total = len(used) * page_limit
    cut = heads * head_size
    width = out_weight.shape[1] // 2
    limit = 16 * 1024 * 1024
    params = pltpu.CompilerParams(vmem_limit_bytes=limit)

    query_rows = jnp.transpose(queries, (1, 0, 2))
    entry_rows = new_entries.reshape(children * 2 * key_heads, head_size)
    scales = jnp.transpose(cache_scales, (1, 2, 0)).reshape(2 * key_heads, page_count)

    send, item_pages, item_lengths, scale_values, select, pages, weight_head = pl.pallas_call(
        functools.partial(pack_kernel, beams, slots, used),
        out_shape=(
            VMEM((beams, slots * ITEM_ROWS, head_size), jnp.bfloat16),
            SMEM((page_total,), jnp.int32),
            SMEM((len(used),), jnp.int32),
            SMEM(scales.shape, jnp.float32),
            VMEM((children, 2 * items), jnp.bfloat16),
            VMEM(cache_pages.shape, jnp.bfloat16),
            VMEM((cut, out_weight.shape[1]), jnp.bfloat16),
        ),
        in_specs=[spec(HBM)] * 9,
        out_specs=(spec(VMEM),) + (spec(SMEM),) * 3 + (spec(VMEM),) * 3,
        scratch_shapes=[
            SMEM(parent.shape, jnp.int32),
            SMEM(placement.shape, jnp.int32),
            VMEM(query_rows.shape, jnp.bfloat16),
            VMEM(entry_rows.shape, jnp.bfloat16),
            SMEM(page_table.shape[::-1], jnp.int32),
            SMEM(lengths.shape, jnp.int32),
            VMEM(scales.shape, jnp.bfloat16),
            VMEM(scales.shape, jnp.float32),
            SMEM((items + 1,), jnp.int32),
            SMEM((beams,), jnp.int32),
            pltpu.SemaphoreType.DMA((10,)),
        ],
        compiler_params=params,
        name="pack",
    )(
        *kept(
            HBM,
            parent,
            placement,
            query_rows,
            entry_rows,
            jnp.transpose(page_table),
            lengths,
            scales,
            cache_pages,
            out_weight,
        )
    )

    arrived = lax.all_to_all(send, "beam", split_axis=0, concat_axis=0, tiled=True)

    partial_sums = pl.pallas_call(
        functools.partial(attend_kernel, slots, used, 1.0 / math.sqrt(head_size)),
        out_shape=VMEM((beams * 2, slots, width), jnp.bfloat16),
        in_specs=[spec(SMEM)] * 3 + [spec(VMEM)] * 3 + [spec(HBM)],
        out_specs=spec(VMEM),
        scratch_shapes=[
            VMEM((16, 128), jnp.bfloat16),
            VMEM((len(used) * ITEM_ROWS, page_limit * page_rows), jnp.float32),
            VMEM((len(used) * ITEM_ROWS, page_limit * page_rows), jnp.bfloat16),
            VMEM((len(used) * ITEM_ROWS, head_size), jnp.float32),
            VMEM((items * ITEM_ROWS, head_size), jnp.float32),
            pltpu.SemaphoreType.DMA((1,)),
        ],
        compiler_params=params,
        name="attend",
    )(
        *kept(SMEM, item_pages, item_lengths, scale_values),
        *kept(VMEM, arrived.reshape(items, ITEM_ROWS, head_size), pages, weight_head),
        *kept(HBM, out_weight),
    )

    returned = lax.all_to_all(partial_sums, ("beam", "tp"), split_axis=0, concat_axis=0, tiled=True)

    return pl.pallas_call(
        finish_kernel,
        out_shape=jax.ShapeDtypeStruct((children, width), jnp.bfloat16),
        in_specs=[spec(VMEM)] * 2,
        out_specs=spec(VMEM),
        compiler_params=params,
        name="finish",
    )(*kept(VMEM, select, returned))


def solution(mesh):
    return jax.shard_map(
        on_device,
        mesh=mesh,
        in_specs=(
            P(("grp", "beam"), "tp", None),
            P(("grp", "beam"), None, "tp", None),
            P(("grp", "beam"), None, "tp", None, None),
            P(("grp", "beam"), None, "tp"),
            P(("grp", "beam"), None),
            P("grp"),
            P("grp"),
            P("grp"),
            P("tp", None),
        ),
        out_specs=P(("grp", "beam"), "tp"),
        check_vma=False,
    )
```

```python
import functools
import math

import jax
import jax.numpy as jnp
from jax import lax
from jax.experimental import pallas as pl
from jax.experimental.pallas import tpu as pltpu
from jax.sharding import PartitionSpec as P

ITEM_ROWS = 16
VMEM = pltpu.VMEM
SMEM = pltpu.SMEM
HBM = pltpu.HBM


def fetch(pairs, sem_ref):
    copies = [pltpu.make_async_copy(a, b, sem_ref.at[i]) for i, (a, b) in enumerate(pairs)]
    for copy in copies:
        copy.start()
    return copies


def pack_kernel(
    beams,
    slots,
    used,
    parent_hbm,
    placement_hbm,
    query_hbm,
    entry_hbm,
    table_hbm,
    length_hbm,
    scale_hbm,
    pages_hbm,
    weight_hbm,
    send_ref,
    page_ref,
    item_length_ref,
    scale_ref,
    select_ref,
    pages_ref,
    weight_ref,
    parent_ref,
    placement_ref,
    query_ref,
    entry_ref,
    table_ref,
    length_ref,
    scale_in_ref,
    scale_wide_ref,
    item_ref,
    asked_ref,
    count_ref,
    sem_ref,
    page_sem_ref,
):
    heads, children, head_size = query_ref.shape
    entry_rows = entry_ref.shape[0]
    per_child = entry_rows // children
    page_limit = table_ref.shape[0]
    copies = fetch(
        [
            (parent_hbm, parent_ref),
            (placement_hbm, placement_ref),
            (query_hbm, query_ref),
            (entry_hbm, entry_ref),
            (table_hbm, table_ref),
            (length_hbm, length_ref),
            (scale_hbm, scale_in_ref),
            (weight_hbm, weight_ref),
        ],
        sem_ref,
    )
    own = lax.axis_index("beam")
    for index in range(beams):
        count_ref[index] = 0
    query_lane = lax.broadcasted_iota(jnp.int32, (8, heads * children), 1)
    entry_lane = lax.broadcasted_iota(jnp.int32, (8, entry_rows), 1)
    query_child = query_lane % children
    entry_child = entry_lane // per_child
    query_row = query_lane // children
    entry_row = entry_lane % per_child + heads
    select_shape = select_ref.shape
    child_row = lax.broadcasted_iota(jnp.int32, select_shape, 0)
    select_lane = lax.broadcasted_iota(jnp.int32, select_shape, 1)
    select_item = (select_lane // (2 * slots)) * slots + select_lane % slots
    wanted = jnp.zeros(select_shape, jnp.int32)
    for copy in (copies[0], copies[1], copies[4], copies[5]):
        copy.wait()

    def one_index(index, _):
        candidates = [placement_ref[parent_ref[index * children + child]] for child in range(children)]
        place = index * slots
        for slot in candidates:
            item_ref[place] = slot % children
            place = place + (slot // children == own).astype(jnp.int32)
        return 0

    for place in range(beams * slots):
        item_ref[place] = 0
    for local in range(children):
        asked_ref[local] = 0
    lax.fori_loop(0, beams, one_index, 0)
    page_rows = pages_ref.shape[3]
    for place, item in enumerate(used):
        local = item_ref[item]
        asked_ref[local] = 1
        length = length_ref[own * children + local]
        item_length_ref[place] = length
        for page in range(page_limit):
            kept_page = jnp.where(page * page_rows < length, page, 0)
            page_ref[place * page_limit + page] = table_ref[kept_page, local]

    def each_asked(act):
        def one_slot(local, _):
            length = length_ref[own * children + local]
            for page in range(page_limit):

                @pl.when((asked_ref[local] > 0) & (page * page_rows < length))
                def _():
                    number = table_ref[page, local]
                    act(
                        pltpu.make_async_copy(
                            pages_hbm.at[number], pages_ref.at[number], page_sem_ref.at[local * page_limit + page]
                        )
                    )

            return 0

        lax.fori_loop(0, children, one_slot, 0)

    each_asked(lambda copy: copy.start())
    own_slots = [placement_ref[parent_ref[own * children + child]] for child in range(children)]
    for child, slot in enumerate(own_slots):
        source = slot // children
        rank = count_ref[source]
        count_ref[source] = rank + 1
        item = source * slots + rank
        wanted = jnp.where(child_row == child, item, wanted)
        first = item * ITEM_ROWS
        query_row = jnp.where(query_child == child, query_row + first, query_row)
        entry_row = jnp.where(entry_child == child, entry_row + first, entry_row)
    rows = beams * slots * ITEM_ROWS
    row_of = lax.broadcasted_iota(jnp.int32, (rows, heads * children), 0)
    pick = (row_of == query_row[:1]).astype(jnp.float32).astype(jnp.bfloat16)
    entry_row_of = lax.broadcasted_iota(jnp.int32, (rows, entry_rows), 0)
    entry_pick = (entry_row_of == entry_row[:1]).astype(jnp.float32).astype(jnp.bfloat16)
    copies[2].wait()
    copies[3].wait()
    moved = jnp.dot(
        pick, query_ref[...].reshape(heads * children, head_size), preferred_element_type=jnp.float32
    )
    moved += jnp.dot(entry_pick, entry_ref[...], preferred_element_type=jnp.float32)
    send_ref[...] = moved.astype(jnp.bfloat16).reshape(send_ref.shape)
    select_ref[...] = (select_item == wanted).astype(jnp.float32).astype(jnp.bfloat16)
    copies[6].wait()
    scale_wide_ref[...] = scale_in_ref[...].astype(jnp.float32)
    scale_copy = pltpu.make_async_copy(scale_wide_ref, scale_ref, sem_ref.at[8])
    scale_copy.start()
    scale_copy.wait()
    copies[7].wait()
    each_asked(lambda copy: copy.wait())


def attend_kernel(
    slots,
    used,
    factor,
    page_ref,
    item_length_ref,
    scale_ref,
    arrived_ref,
    pages_ref,
    weight_ref,
    out_ref,
    score_ref,
    rounded_ref,
    denominator_ref,
    attended_ref,
):
    item_count = arrived_ref.shape[0]
    _, _, key_heads, page_rows, head_size = pages_ref.shape
    page_limit = page_ref.shape[0] // len(used)
    heads = weight_ref.shape[0] // head_size
    group = heads // key_heads
    row = lax.broadcasted_iota(jnp.int32, (ITEM_ROWS, head_size), 0)
    row_head = [(row >= head * group) & (row < (head + 1) * group) for head in range(key_heads)]

    def by_head(parts):
        result = jnp.zeros((ITEM_ROWS, head_size), jnp.float32)
        for mask, part in zip(row_head, parts):
            result = jnp.where(mask, part, result)
        return result

    def rows_of(item):
        return slice(item * ITEM_ROWS, (item + 1) * ITEM_ROWS)

    def both_heads(number, which):
        return jnp.concatenate([pages_ref[number, which, head] for head in range(key_heads)], axis=1)

    def scores_of(place, item):
        packed = arrived_ref[item].astype(jnp.float32)
        wide = jnp.concatenate([jnp.where(mask, packed, 0.0) for mask in row_head], axis=1).astype(jnp.bfloat16)
        length = item_length_ref[place]
        for page in range(page_limit):
            number = page_ref[place * page_limit + page]
            raw = lax.dot_general(
                wide, both_heads(number, 0), (((1,), (1,)), ((), ())), preferred_element_type=jnp.float32
            )
            key_scale = by_head([scale_ref[head, number] * factor for head in range(key_heads)])
            hidden = jnp.where(page * page_rows < length, 0.0, -jnp.inf)
            score_ref[rows_of(place), page * page_rows : (page + 1) * page_rows] = raw * key_scale + hidden

    def weights_of(place, item):
        packed = arrived_ref[item].astype(jnp.float32)
        fresh_key = by_head([packed[heads + head][None] for head in range(key_heads)])
        fresh_value = by_head([packed[heads + key_heads + head][None] for head in range(key_heads)])
        scores = score_ref[rows_of(place), :]
        fresh = jnp.sum(packed * fresh_key, axis=1, keepdims=True) * factor
        highest = jnp.maximum(jnp.max(scores, axis=1, keepdims=True), fresh)
        fresh_weight = jnp.exp(fresh - highest)
        weights = jnp.exp(scores - highest)
        rounded_ref[rows_of(place), :] = weights.astype(jnp.bfloat16)
        denominator = jnp.sum(weights, axis=1, keepdims=True) + fresh_weight
        denominator_ref[rows_of(place), :] = jnp.broadcast_to(denominator, (ITEM_ROWS, head_size))
        attended_ref[rows_of(item), :] = fresh_weight.astype(jnp.bfloat16).astype(jnp.float32) * fresh_value

    def values_of(place, item):
        summed = attended_ref[rows_of(item), :]
        for page in range(page_limit):
            number = page_ref[place * page_limit + page]
            product = jnp.dot(
                rounded_ref[rows_of(place), page * page_rows : (page + 1) * page_rows],
                both_heads(number, 1),
                preferred_element_type=jnp.float32,
            )
            summed = summed + by_head(
                [
                    product[:, head * head_size : (head + 1) * head_size] * scale_ref[key_heads + head, number]
                    for head in range(key_heads)
                ],
            )
        attended_ref[rows_of(item), :] = summed / denominator_ref[rows_of(place), :]

    if len(used) < item_count:
        attended_ref[...] = jnp.zeros_like(attended_ref)
    for step in (scores_of, weights_of, values_of):
        for place, item in enumerate(used):
            step(place, item)
    attended = jnp.concatenate(
        [attended_ref[pl.ds(head, item_count, stride=ITEM_ROWS), :] for head in range(heads)], axis=1
    ).astype(jnp.bfloat16)
    total = jnp.dot(attended, weight_ref[...], preferred_element_type=jnp.float32)
    total = total.astype(jnp.bfloat16)
    width = out_ref.shape[2]
    for half in range(2):
        for index in range(item_count // slots):
            out_ref[index * 2 + half] = total[index * slots : (index + 1) * slots, half * width : (half + 1) * width]


def finish_kernel(select_ref, arrived_ref, out_ref):
    members, slots, width = arrived_ref.shape
    parts = arrived_ref[...].reshape(members * slots, width)
    out_ref[...] = jnp.dot(select_ref[...], parts, preferred_element_type=jnp.float32).astype(out_ref.dtype)


def kept(space, *arrays):
    return tuple(pltpu.with_memory_space_constraint(array, space) for array in arrays)


def spec(space):
    return pl.BlockSpec(memory_space=space)


def on_device(
    queries,
    new_entries,
    cache_pages,
    cache_scales,
    page_table,
    lengths,
    parent,
    placement,
    out_weight,
):
    beams = lax.axis_size("beam")
    children, heads, head_size = queries.shape
    key_heads = new_entries.shape[2]
    page_limit = page_table.shape[1]
    page_count = cache_pages.shape[0]
    page_rows = cache_pages.shape[3]
    wanted = (children + beams - 1) // beams
    slots = wanted + wanted % 2
    items = beams * slots
    used = [index * slots + rank for index in range(beams) for rank in range(wanted)]
    page_total = len(used) * page_limit
    width = out_weight.shape[1] // 2
    limit = 16 * 1024 * 1024
    params = pltpu.CompilerParams(vmem_limit_bytes=limit)

    query_rows = jnp.transpose(queries, (1, 0, 2))
    entry_rows = new_entries.reshape(children * 2 * key_heads, head_size)
    scales = jnp.transpose(cache_scales, (1, 2, 0)).reshape(2 * key_heads, page_count)

    send, item_pages, item_lengths, scale_values, select, pages, weight = pl.pallas_call(
        functools.partial(pack_kernel, beams, slots, used),
        out_shape=(
            VMEM((beams, slots * ITEM_ROWS, head_size), jnp.bfloat16),
            SMEM((page_total,), jnp.int32),
            SMEM((len(used),), jnp.int32),
            SMEM(scales.shape, jnp.float32),
            VMEM((children, 2 * items), jnp.bfloat16),
            VMEM(cache_pages.shape, jnp.bfloat16),
            VMEM(out_weight.shape, jnp.bfloat16),
        ),
        in_specs=[spec(HBM)] * 9,
        out_specs=(spec(VMEM),) + (spec(SMEM),) * 3 + (spec(VMEM),) * 3,
        scratch_shapes=[
            SMEM(parent.shape, jnp.int32),
            SMEM(placement.shape, jnp.int32),
            VMEM(query_rows.shape, jnp.bfloat16),
            VMEM(entry_rows.shape, jnp.bfloat16),
            SMEM(page_table.shape[::-1], jnp.int32),
            SMEM(lengths.shape, jnp.int32),
            VMEM(scales.shape, jnp.bfloat16),
            VMEM(scales.shape, jnp.float32),
            SMEM((items + 1,), jnp.int32),
            SMEM((children,), jnp.int32),
            SMEM((beams,), jnp.int32),
            pltpu.SemaphoreType.DMA((9,)),
            pltpu.SemaphoreType.DMA((children * page_limit,)),
        ],
        compiler_params=params,
        name="pack",
    )(
        *kept(
            HBM,
            parent,
            placement,
            query_rows,
            entry_rows,
            jnp.transpose(page_table),
            lengths,
            scales,
            cache_pages,
            out_weight,
        )
    )

    arrived = lax.all_to_all(send, "beam", split_axis=0, concat_axis=0, tiled=True)

    partial_sums = pl.pallas_call(
        functools.partial(attend_kernel, slots, used, 1.0 / math.sqrt(head_size)),
        out_shape=VMEM((beams * 2, slots, width), jnp.bfloat16),
        in_specs=[spec(SMEM)] * 3 + [spec(VMEM)] * 3,
        out_specs=spec(VMEM),
        scratch_shapes=[
            VMEM((len(used) * ITEM_ROWS, page_limit * page_rows), jnp.float32),
            VMEM((len(used) * ITEM_ROWS, page_limit * page_rows), jnp.bfloat16),
            VMEM((len(used) * ITEM_ROWS, head_size), jnp.float32),
            VMEM((items * ITEM_ROWS, head_size), jnp.float32),
        ],
        compiler_params=params,
        name="attend",
    )(
        *kept(SMEM, item_pages, item_lengths, scale_values),
        *kept(VMEM, arrived.reshape(items, ITEM_ROWS, head_size), pages, weight),
    )

    returned = lax.all_to_all(partial_sums, ("beam", "tp"), split_axis=0, concat_axis=0, tiled=True)

    return pl.pallas_call(
        finish_kernel,
        out_shape=jax.ShapeDtypeStruct((children, width), jnp.bfloat16),
        in_specs=[spec(VMEM)] * 2,
        out_specs=spec(VMEM),
        compiler_params=params,
        name="finish",
    )(*kept(VMEM, select, returned))


def solution(mesh):
    return jax.shard_map(
        on_device,
        mesh=mesh,
        in_specs=(
            P(("grp", "beam"), "tp", None),
            P(("grp", "beam"), None, "tp", None),
            P(("grp", "beam"), None, "tp", None, None),
            P(("grp", "beam"), None, "tp"),
            P(("grp", "beam"), None),
            P("grp"),
            P("grp"),
            P("grp"),
            P("tp", None),
        ),
        out_specs=P(("grp", "beam"), "tp"),
        check_vma=False,
    )
```

```python
import functools
import math

import jax
import jax.numpy as jnp
from jax import lax
from jax.experimental import pallas as pl
from jax.experimental.pallas import tpu as pltpu
from jax.sharding import PartitionSpec as P

ITEM_ROWS = 16
VMEM = pltpu.VMEM
SMEM = pltpu.SMEM
HBM = pltpu.HBM


def fetch(pairs, sem_ref):
    copies = [pltpu.make_async_copy(a, b, sem_ref.at[i]) for i, (a, b) in enumerate(pairs)]
    for copy in copies:
        copy.start()
    return copies


def pack_kernel(
    beams,
    slots,
    used,
    parent_hbm,
    placement_hbm,
    query_hbm,
    entry_hbm,
    table_hbm,
    length_hbm,
    scale_hbm,
    pages_hbm,
    send_ref,
    page_ref,
    item_length_ref,
    scale_ref,
    select_ref,
    pages_ref,
    parent_ref,
    placement_ref,
    query_ref,
    entry_ref,
    table_ref,
    length_ref,
    scale_in_ref,
    scale_wide_ref,
    item_ref,
    count_ref,
    sem_ref,
):
    heads, children, head_size = query_ref.shape
    entry_rows = entry_ref.shape[0]
    per_child = entry_rows // children
    page_limit = table_ref.shape[0]
    copies = fetch(
        [
            (parent_hbm, parent_ref),
            (placement_hbm, placement_ref),
            (query_hbm, query_ref),
            (entry_hbm, entry_ref),
            (table_hbm, table_ref),
            (length_hbm, length_ref),
            (scale_hbm, scale_in_ref),
            (pages_hbm, pages_ref),
        ],
        sem_ref,
    )
    own = lax.axis_index("beam")
    for index in range(beams):
        count_ref[index] = 0
    query_lane = lax.broadcasted_iota(jnp.int32, (8, heads * children), 1)
    entry_lane = lax.broadcasted_iota(jnp.int32, (8, entry_rows), 1)
    query_child = query_lane % children
    entry_child = entry_lane // per_child
    query_row = query_lane // children
    entry_row = entry_lane % per_child + heads
    select_shape = select_ref.shape
    select_row = lax.broadcasted_iota(jnp.int32, select_shape, 0)
    child_row = select_row % children
    select_lane = lax.broadcasted_iota(jnp.int32, select_shape, 1)
    select_item = (select_lane // (2 * slots)) * slots + select_lane % slots
    wanted = jnp.zeros(select_shape, jnp.int32)
    copies[0].wait()
    copies[1].wait()
    own_slots = [placement_ref[parent_ref[own * children + child]] for child in range(children)]
    for child, slot in enumerate(own_slots):
        source = slot // children
        rank = count_ref[source]
        count_ref[source] = rank + 1
        item = source * slots + rank
        wanted = jnp.where(child_row == child, item, wanted)
        first = item * ITEM_ROWS
        query_row = jnp.where(query_child == child, query_row + first, query_row)
        entry_row = jnp.where(entry_child == child, entry_row + first, entry_row)
    rows = beams * slots * ITEM_ROWS
    row_of = lax.broadcasted_iota(jnp.int32, (rows, heads * children), 0)
    pick = (row_of == query_row[:1]).astype(jnp.float32).astype(jnp.bfloat16)
    entry_row_of = lax.broadcasted_iota(jnp.int32, (rows, entry_rows), 0)
    entry_pick = (entry_row_of == entry_row[:1]).astype(jnp.float32).astype(jnp.bfloat16)
    copies[2].wait()
    copies[3].wait()
    moved = jnp.dot(
        pick, query_ref[...].reshape(heads * children, head_size), preferred_element_type=jnp.float32
    )
    moved += jnp.dot(entry_pick, entry_ref[...], preferred_element_type=jnp.float32)
    send_ref[...] = moved.astype(jnp.bfloat16).reshape(send_ref.shape)
    picked = (select_item == wanted) & ((select_lane // slots) % 2 == select_row // children)
    select_ref[...] = picked.astype(jnp.float32).astype(jnp.bfloat16)
    copies[6].wait()
    scale_wide_ref[...] = scale_in_ref[...].astype(jnp.float32)
    scale_copy = pltpu.make_async_copy(scale_wide_ref, scale_ref, sem_ref.at[8])
    scale_copy.start()

    def one_index(index, _):
        asked = [placement_ref[parent_ref[index * children + child]] for child in range(children)]
        place = index * slots
        for slot in asked:
            item_ref[place] = slot % children
            place = place + (slot // children == own).astype(jnp.int32)
        return 0

    lax.fori_loop(0, beams, one_index, 0)
    copies[4].wait()
    copies[5].wait()
    for place, item in enumerate(used):
        local = item_ref[item]
        item_length_ref[place] = length_ref[own * children + local]
        for page in range(page_limit):
            page_ref[place * page_limit + page] = table_ref[page, local]
    scale_copy.wait()
    copies[7].wait()


def attend_kernel(
    slots,
    used,
    factor,
    page_ref,
    item_length_ref,
    scale_ref,
    arrived_ref,
    pages_ref,
    out_ref,
    score_ref,
    rounded_ref,
    denominator_ref,
    attended_ref,
):
    item_count = arrived_ref.shape[0]
    _, _, key_heads, page_rows, head_size = pages_ref.shape
    page_limit = page_ref.shape[0] // len(used)
    heads = out_ref.shape[2] // head_size
    group = heads // key_heads
    row = lax.broadcasted_iota(jnp.int32, (ITEM_ROWS, head_size), 0)
    row_head = [(row >= head * group) & (row < (head + 1) * group) for head in range(key_heads)]

    def by_head(parts):
        result = jnp.zeros((ITEM_ROWS, head_size), jnp.float32)
        for mask, part in zip(row_head, parts):
            result = jnp.where(mask, part, result)
        return result

    def rows_of(item):
        return slice(item * ITEM_ROWS, (item + 1) * ITEM_ROWS)

    def both_heads(number, which):
        return jnp.concatenate([pages_ref[number, which, head] for head in range(key_heads)], axis=1)

    def scores_of(place, item):
        packed = arrived_ref[item].astype(jnp.float32)
        wide = jnp.concatenate([jnp.where(mask, packed, 0.0) for mask in row_head], axis=1).astype(jnp.bfloat16)
        length = item_length_ref[place]
        for page in range(page_limit):
            number = page_ref[place * page_limit + page]
            raw = lax.dot_general(
                wide, both_heads(number, 0), (((1,), (1,)), ((), ())), preferred_element_type=jnp.float32
            )
            key_scale = by_head([scale_ref[head, number] * factor for head in range(key_heads)])
            hidden = jnp.where(page * page_rows < length, 0.0, -jnp.inf)
            score_ref[rows_of(place), page * page_rows : (page + 1) * page_rows] = raw * key_scale + hidden

    def weights_of(place, item):
        packed = arrived_ref[item].astype(jnp.float32)
        fresh_key = by_head([packed[heads + head][None] for head in range(key_heads)])
        fresh_value = by_head([packed[heads + key_heads + head][None] for head in range(key_heads)])
        scores = score_ref[rows_of(place), :]
        fresh = jnp.sum(packed * fresh_key, axis=1, keepdims=True) * factor
        highest = jnp.maximum(jnp.max(scores, axis=1, keepdims=True), fresh)
        fresh_weight = jnp.exp(fresh - highest)
        weights = jnp.exp(scores - highest)
        rounded_ref[rows_of(place), :] = weights.astype(jnp.bfloat16)
        denominator = jnp.sum(weights, axis=1, keepdims=True) + fresh_weight
        denominator_ref[rows_of(place), :] = jnp.broadcast_to(denominator, (ITEM_ROWS, head_size))
        attended_ref[rows_of(item), :] = fresh_weight.astype(jnp.bfloat16).astype(jnp.float32) * fresh_value

    def values_of(place, item):
        summed = attended_ref[rows_of(item), :]
        for page in range(page_limit):
            number = page_ref[place * page_limit + page]
            product = jnp.dot(
                rounded_ref[rows_of(place), page * page_rows : (page + 1) * page_rows],
                both_heads(number, 1),
                preferred_element_type=jnp.float32,
            )
            summed = summed + by_head(
                [
                    product[:, head * head_size : (head + 1) * head_size] * scale_ref[key_heads + head, number]
                    for head in range(key_heads)
                ],
            )
        attended_ref[rows_of(item), :] = summed / denominator_ref[rows_of(place), :]

    if len(used) < item_count:
        attended_ref[...] = jnp.zeros_like(attended_ref)
    for step in (scores_of, weights_of, values_of):
        for place, item in enumerate(used):
            step(place, item)
    attended = jnp.concatenate(
        [attended_ref[pl.ds(head, item_count, stride=ITEM_ROWS), :] for head in range(heads)], axis=1
    ).astype(jnp.bfloat16)
    for half in range(2):
        for index in range(item_count // slots):
            out_ref[index * 2 + half] = attended[index * slots : (index + 1) * slots]


def finish_kernel(select_ref, arrived_ref, own_weight_ref, other_weight_ref, out_ref):
    members, slots, depth = arrived_ref.shape
    children, width = out_ref.shape
    parts = arrived_ref[...].reshape(members * slots, depth)
    ordered = jnp.dot(select_ref[...], parts, preferred_element_type=jnp.float32).astype(jnp.bfloat16)
    half = lax.axis_index("tp")
    low, high = ordered[:children], ordered[children:]
    own = jnp.where(half == 0, low, high)
    other = jnp.where(half == 0, high, low)
    columns = pl.ds(pl.multiple_of(half * width, 128), width)
    total = jnp.dot(own, own_weight_ref[:, columns], preferred_element_type=jnp.float32)
    total += jnp.dot(other, other_weight_ref[:, columns], preferred_element_type=jnp.float32)
    out_ref[...] = total.astype(out_ref.dtype)


def kept(space, *arrays):
    return tuple(pltpu.with_memory_space_constraint(array, space) for array in arrays)


def spec(space):
    return pl.BlockSpec(memory_space=space)


def on_device(
    queries,
    new_entries,
    cache_pages,
    cache_scales,
    page_table,
    lengths,
    parent,
    placement,
    out_weight,
):
    beams = lax.axis_size("beam")
    children, heads, head_size = queries.shape
    key_heads = new_entries.shape[2]
    page_limit = page_table.shape[1]
    page_count = cache_pages.shape[0]
    page_rows = cache_pages.shape[3]
    wanted = (children + beams - 1) // beams
    slots = wanted + wanted % 2
    items = beams * slots
    used = [index * slots + rank for index in range(beams) for rank in range(wanted)]
    page_total = len(used) * page_limit
    width = out_weight.shape[1] // 2
    limit = 16 * 1024 * 1024
    params = pltpu.CompilerParams(vmem_limit_bytes=limit)

    query_rows = jnp.transpose(queries, (1, 0, 2))
    entry_rows = new_entries.reshape(children * 2 * key_heads, head_size)
    scales = jnp.transpose(cache_scales, (1, 2, 0)).reshape(2 * key_heads, page_count)

    swap = [(half, 1 - half) for half in range(2)]
    other_weight = lax.ppermute(out_weight, "tp", swap)
    send, item_pages, item_lengths, scale_values, select, pages = pl.pallas_call(
        functools.partial(pack_kernel, beams, slots, used),
        out_shape=(
            VMEM((beams, slots * ITEM_ROWS, head_size), jnp.bfloat16),
            SMEM((page_total,), jnp.int32),
            SMEM((len(used),), jnp.int32),
            SMEM(scales.shape, jnp.float32),
            VMEM((2 * children, 2 * items), jnp.bfloat16),
            VMEM(cache_pages.shape, jnp.bfloat16),
        ),
        in_specs=[spec(HBM)] * 8,
        out_specs=(spec(VMEM),) + (spec(SMEM),) * 3 + (spec(VMEM),) * 2,
        scratch_shapes=[
            SMEM(parent.shape, jnp.int32),
            SMEM(placement.shape, jnp.int32),
            VMEM(query_rows.shape, jnp.bfloat16),
            VMEM(entry_rows.shape, jnp.bfloat16),
            SMEM(page_table.shape[::-1], jnp.int32),
            SMEM(lengths.shape, jnp.int32),
            VMEM(scales.shape, jnp.bfloat16),
            VMEM(scales.shape, jnp.float32),
            SMEM((items + 1,), jnp.int32),
            SMEM((beams,), jnp.int32),
            pltpu.SemaphoreType.DMA((9,)),
        ],
        compiler_params=params,
        name="pack",
    )(
        *kept(
            HBM,
            parent,
            placement,
            query_rows,
            entry_rows,
            jnp.transpose(page_table),
            lengths,
            scales,
            cache_pages,
        )
    )

    arrived = lax.all_to_all(send, "beam", split_axis=0, concat_axis=0, tiled=True)

    arrived, sent_back = lax.optimization_barrier((arrived, other_weight))
    own_weight = lax.ppermute(sent_back, "tp", swap)
    attended = pl.pallas_call(
        functools.partial(attend_kernel, slots, used, 1.0 / math.sqrt(head_size)),
        out_shape=VMEM((beams * 2, slots, heads * head_size), jnp.bfloat16),
        in_specs=[spec(SMEM)] * 3 + [spec(VMEM)] * 2,
        out_specs=spec(VMEM),
        scratch_shapes=[
            VMEM((len(used) * ITEM_ROWS, page_limit * page_rows), jnp.float32),
            VMEM((len(used) * ITEM_ROWS, page_limit * page_rows), jnp.bfloat16),
            VMEM((len(used) * ITEM_ROWS, head_size), jnp.float32),
            VMEM((items * ITEM_ROWS, head_size), jnp.float32),
        ],
        compiler_params=params,
        name="attend",
    )(
        *kept(SMEM, item_pages, item_lengths, scale_values),
        *kept(VMEM, arrived.reshape(items, ITEM_ROWS, head_size), pages),
    )

    returned = lax.all_to_all(attended, ("beam", "tp"), split_axis=0, concat_axis=0, tiled=True)

    return pl.pallas_call(
        finish_kernel,
        out_shape=jax.ShapeDtypeStruct((children, width), jnp.bfloat16),
        in_specs=[spec(VMEM)] * 4,
        out_specs=spec(VMEM),
        compiler_params=params,
        name="finish",
    )(*kept(VMEM, select, returned, own_weight, other_weight))


def solution(mesh):
    return jax.shard_map(
        on_device,
        mesh=mesh,
        in_specs=(
            P(("grp", "beam"), "tp", None),
            P(("grp", "beam"), None, "tp", None),
            P(("grp", "beam"), None, "tp", None, None),
            P(("grp", "beam"), None, "tp"),
            P(("grp", "beam"), None),
            P("grp"),
            P("grp"),
            P("grp"),
            P("tp", None),
        ),
        out_specs=P(("grp", "beam"), "tp"),
        check_vma=False,
    )
```
